256 devices in a mesh: seq: 32 (over y, z_hi, x), tower: 8 (over z_lo, core).
Axes of the slice: x: 4, y: 4, z: 8 (z_hi: 2, z_lo: 4; z = z_hi * 4 + z_lo), core: 2. Of those that a mesh axis runs over, the one named last changes fastest.
Arguments:
- q_self: bfloat16 [8, 3072, 3072], P('tower', 'seq'), may hold values from -6 to 6
- k_self: bfloat16 [8, 3072, 3072], P('tower', 'seq'), may hold values from -6 to 6
- v_self: bfloat16 [8, 3072, 3072], P('tower', 'seq'), may hold values from -6 to 6
- q_cross: bfloat16 [8, 3072, 3072], P('tower', 'seq'), may hold values from -12 to 12
- k_cross: bfloat16 [8, 3072, 3072], P('tower', 'seq'), may hold values from -8 to 8
- v_cross: bfloat16 [8, 3072, 3072], P('tower', 'seq'), may hold values from -8 to 8
- scale_exps: int32 [8, 2, 24], P('tower'), may hold values from -8 to -5
- cross_slopes: float32 [2, 24], replicated, may hold values from 0.5 to 16
- offsets: int32 [8], replicated, may hold values from 0 to 1535
Outputs:
- self_out: bfloat16 [8, 3072, 3072], P('tower', 'seq')
- cross_out: bfloat16 [8, 3072, 3072], P('tower', 'seq')
The draws below stay inside these ranges and needn't reach their ends.
All inputs are finite; a program needn't handle non-finite values.
Results may differ from the reference program's by a relative error of at most 0.0049.
Values may be sent and summed in bfloat16 or wider, within the bound.
No kernel may reach another device: no remote copies, remote signals or barrier semaphores. Data moves between devices by JAX's collectives and lax.ppermute only.
A program may use at most 64 MiB of HBM per device.

```python
import math
import jax
import jax.numpy as jnp
from jax import lax

HEADS = 24
HD = 128
D = 3072
TOKENS = 3072
N_TOWER = 8


def planted_pair(base_key, salt_value, query_top, key_top, key_scale, paired):
    base_key = jax.random.fold_in(base_key, salt_value)
    streams = jax.random.split(base_key, 5)
    feature_count = HEADS * HD
    array_shape = (N_TOWER, TOKENS, feature_count)
    queries = jnp.clip(jax.random.normal(streams[0], array_shape, jnp.float32), -query_top, query_top)
    key_rows = jnp.clip(key_scale * jax.random.normal(streams[1], array_shape, jnp.float32), -key_top, key_top)
    planted = 4
    owners = jnp.broadcast_to(jnp.arange(N_TOWER, dtype=jnp.int32)[:, None], (N_TOWER, planted))
    key_owners = jnp.bitwise_xor(owners, N_TOWER // 2 * paired)
    at_query = jax.random.randint(streams[2], (N_TOWER, planted), 0, TOKENS)
    at_first = jax.random.randint(streams[3], (N_TOWER, planted), 0, TOKENS)
    at_second = (at_first + 1 + jax.random.randint(streams[4], (N_TOWER, planted), 0, TOKENS - 1)) % TOKENS
    queries = queries.at[owners, at_query].set(queries[owners, at_query])
    key_rows = key_rows.at[key_owners, at_first].set(key_rows[key_owners, at_first])
    key_rows = key_rows.at[key_owners, at_second].set(key_rows[key_owners, at_second])
    return (queries, key_rows)


def draw_q_self(key, part):
    return planted_pair(key, 11, 6.0, 6.0, 1.0, 0)[0].astype(jnp.bfloat16)


def draw_k_self(key, part):
    return planted_pair(key, 11, 6.0, 6.0, 1.0, 0)[1].astype(jnp.bfloat16)


def draw_q_cross(key, part):
    return planted_pair(key, 23, 12.0, 8.0, 2.0, 1)[0].astype(jnp.bfloat16)


def draw_k_cross(key, part):
    return planted_pair(key, 23, 12.0, 8.0, 2.0, 1)[1].astype(jnp.bfloat16)


def plant(result, own_key, least, largest):
    longest = result.shape.index(max(result.shape))
    spots = []
    for shift in (0, 1):
        where = [jax.random.randint(jax.random.fold_in(own_key, axis), (), 0, length) for axis, length in enumerate(result.shape)]
        where[longest] = (where[longest] + shift) % result.shape[longest]
        spots.append(tuple(where))
    return result.at[spots[0]].set(least).at[spots[1]].set(largest)


def block_levels(own_key, dims, cuts, least, high):
    factor_of = 1.0
    for position, shards_of in cuts:
        steps = jax.random.uniform(jax.random.fold_in(jax.random.fold_in(own_key, 6), position), (shards_of,), jnp.float32, least / len(cuts), high / len(cuts))
        factor_of = factor_of * jnp.repeat(jnp.exp(steps), dims[position] // shards_of).reshape((-1,) + (1,) * (len(dims) - 1 - position))
    return factor_of


def scatter_about(stream_key, dims, scale, reach, shards=(), held_as=jnp.bfloat16):
    factor_of = block_levels(stream_key, dims, shards, -0.22, 0.18) if shards else 1.0
    values = jax.random.normal(stream_key, dims, jnp.float32) * scale * factor_of
    return jnp.minimum(jnp.maximum(values, -reach), reach).astype(held_as)


def setup_inputs(seed: int = 0) -> dict:
    streams_of = jax.random.split(jax.random.key(seed), 10)
    return {
        "q_self": draw_q_self(jax.random.fold_in(streams_of[9], 71), 0),
        "k_self": draw_k_self(jax.random.fold_in(streams_of[9], 71), 0),
        "v_self": scatter_about(streams_of[2], (N_TOWER, TOKENS, D), 1.0, 6.0, ((0, 8), (1, 32))),
        "q_cross": draw_q_cross(jax.random.fold_in(streams_of[9], 71), 0),
        "k_cross": draw_k_cross(jax.random.fold_in(streams_of[9], 71), 0),
        "v_cross": scatter_about(streams_of[5], (N_TOWER, TOKENS, D), 2.0, 8.0, ((0, 8), (1, 32))),
        "scale_exps": plant(jax.random.randint(streams_of[6], (N_TOWER, 2, HEADS), -8, -4), jax.random.fold_in(streams_of[6], 1), -8, (-4) - 1).astype(jnp.int32),
        "cross_slopes": jnp.clip(jnp.exp(jax.random.uniform(streams_of[7], (2, HEADS), jnp.float32, math.log(0.5), math.log(16.0))), 0.5, 16.0),
        "offsets": plant(jax.random.randint(streams_of[8], (N_TOWER,), 0, TOKENS // 2), jax.random.fold_in(streams_of[8], 1), 0, (TOKENS // 2) - 1).astype(jnp.int32),
    }


clip_top = 448.0


def softmax_rows(scores):
    row_peak = jnp.max(scores, axis=1, keepdims=True)
    lifted = jnp.exp(scores - row_peak)
    return lifted / jnp.sum(lifted, axis=1, keepdims=True)


def flatten(matrix):
    towers = matrix.shape[0]
    return matrix.reshape(towers, TOKENS, HEADS, HD).transpose(0, 2, 1, 3).reshape(towers * HEADS, TOKENS, HD)


def back_rows(stacked, towers):
    return stacked.reshape(towers, HEADS, TOKENS, HD).transpose(0, 2, 1, 3).reshape(towers, TOKENS, HEADS * HD)


def reference(q_self, k_self, v_self, q_cross, k_cross, v_cross, scale_exps, cross_slopes, offsets):
    towers = q_self.shape[0]
    half_count = towers // 2
    inv_root = HD ** -0.5

    def self_one(packed):
        queries, key_rows, value_rows = packed
        scores = jnp.dot(queries, key_rows.T, preferred_element_type=jnp.float32) * inv_root
        weights = softmax_rows(scores).astype(jnp.bfloat16)
        return jnp.dot(weights, value_rows, preferred_element_type=jnp.float32).astype(jnp.bfloat16)

    self_out = back_rows(lax.map(self_one, (flatten(q_self), flatten(k_self), flatten(v_self))), towers)

    tower_ids = jnp.arange(towers, dtype=jnp.int32)
    partner = jnp.bitwise_xor(tower_ids, half_count)
    powers = scale_exps[partner].astype(jnp.float32)

    def decode(matrix, power):
        widened = matrix[partner].reshape(towers, TOKENS, HEADS, HD).astype(jnp.float32)
        code_vals = jnp.clip(widened * jnp.exp2(-power)[:, None, :, None], -clip_top, clip_top).astype(jnp.bfloat16)
        restored = (code_vals.astype(jnp.float32) * jnp.exp2(power)[:, None, :, None]).astype(jnp.bfloat16)
        return restored.reshape(towers, TOKENS, HEADS * HD)

    keys_back = decode(k_cross, powers[:, 0])
    values_back = decode(v_cross, powers[:, 1])
    positions = jnp.arange(TOKENS, dtype=jnp.int32)
    slopes = cross_slopes[tower_ids // half_count].reshape(towers * HEADS)
    shifts = jnp.repeat(offsets - offsets[partner], HEADS)

    def cross_one(packed):
        queries, key_rows, value_rows, slope_rate, time_shift = packed
        scores = jnp.dot(queries, key_rows.T, preferred_element_type=jnp.float32) * inv_root
        distance = jnp.abs(positions[:, None] + time_shift - positions[None, :]).astype(jnp.float32)
        scores = scores - slope_rate * (distance / TOKENS)
        weights = softmax_rows(scores).astype(jnp.bfloat16)
        return jnp.dot(weights, value_rows, preferred_element_type=jnp.float32).astype(jnp.bfloat16)

    cross_out = back_rows(lax.map(cross_one, (flatten(q_cross), flatten(keys_back), flatten(values_back), slopes, shifts)), towers)
    return self_out, cross_out
```

```python
import functools

import jax
import jax.numpy as jnp
import numpy as np
from jax import lax
from jax.experimental import pallas as pl
from jax.experimental.pallas import tpu as pltpu
from jax.sharding import PartitionSpec as P

HEADS = 24
HD = 128
TOP = 448.0
LOG2E = 1.4426950408889634

NY, NH, NX, NZ = 4, 2, 4, 4
SEATS = NY * NX
HALF = SEATS // 2
PER = HEADS // HALF
BOTH = ("seq", "tower")


def z_route(pick):
    pairs = []
    around = NH * NZ
    for y in range(NY):
        for x in range(NX):
            for z in range(around):
                for core in range(2):

                    def device(at):
                        return (y * NH * NX + (at // NZ) * NX + x) * (2 * NZ) + (at % NZ) * 2 + core

                    pairs.append((device(z), device((z + pick(y * NX + x)) % around)))
    return pairs


def move(block, pick):
    return lax.ppermute(block, BOTH, z_route(pick))


def spread(block):
    groups = [[y * NH * NX + h * NX + x for y in range(NY) for x in range(NX)] for h in range(NH)]
    return lax.all_to_all(block, "seq", 0, 0, axis_index_groups=groups, tiled=True)


def attend_body(slope_ref, base_ref, q_ref, first_ref, second_ref, out_ref, tile_ref, score_ref, *, chunk, run, runs):
    step = pl.program_id(0)
    slope = slope_ref[chunk]

    @pl.when(step == 0)
    def _():
        rows = lax.broadcasted_iota(jnp.int32, (run, run), 0)
        cols = lax.broadcasted_iota(jnp.int32, (run, run), 1)
        tile_ref[...] = (rows - cols).astype(jnp.float32) * slope

    queries = q_ref[...]
    scale = HD ** (-0.5) * LOG2E
    peak = None
    for half, ref in enumerate((first_ref, second_ref)):
        for j in range(runs):
            scores = lax.dot_general(
                queries, ref[j * run : (j + 1) * run, :HD], (((1,), (1,)), ((), ())),
                preferred_element_type=jnp.float32,
            )
            base = ((step - j) * (2 * run) + base_ref[half]).astype(jnp.float32) * slope
            scores = scores * scale - jnp.abs(tile_ref[...] + base)
            at = (half * runs + j) * run
            score_ref[:, at : at + run] = scores
            for lane in range(0, run, 128):
                part = scores[:, lane : lane + 128]
                peak = part if peak is None else jnp.maximum(peak, part)
    peak = jnp.max(peak, axis=1, keepdims=True)
    total = jnp.zeros((run, 128), jnp.float32)
    out = jnp.zeros((run, HD), jnp.float32)
    for half, ref in enumerate((first_ref, second_ref)):
        for j in range(runs):
            at = (half * runs + j) * run
            weights = jnp.exp2(score_ref[:, at : at + run] - peak)
            for lane in range(0, run, 128):
                total = total + weights[:, lane : lane + 128]
            out = out + jnp.dot(
                weights.astype(jnp.bfloat16), ref[j * run : (j + 1) * run, HD:],
                preferred_element_type=jnp.float32,
            )
    out_ref[...] = (out / jnp.sum(total, axis=1, keepdims=True)).astype(jnp.bfloat16)


def attend(slopes, bases, queries, first, second, chunk):
    rows = queries.shape[0]
    runs = NY
    run = rows // runs
    whole = pl.BlockSpec((rows, 2 * HD), lambda i: (0, 0))
    return pl.pallas_call(
        functools.partial(attend_body, chunk=chunk, run=run, runs=runs),
        grid=(runs,),
        in_specs=[
            pl.BlockSpec(memory_space=pltpu.SMEM),
            pl.BlockSpec(memory_space=pltpu.SMEM),
            pl.BlockSpec((run, HD), lambda i: (i, chunk)),
            whole,
            whole,
        ],
        out_specs=pl.BlockSpec((run, HD), lambda i: (i, 0)),
        out_shape=jax.ShapeDtypeStruct((rows, HD), jnp.bfloat16),
        scratch_shapes=[
            pltpu.VMEM((run, run), jnp.float32),
            pltpu.VMEM((run, 2 * rows), jnp.float32),
        ],
        compiler_params=pltpu.CompilerParams(vmem_limit_bytes=32 * 1024 * 1024),
        cost_estimate=pl.CostEstimate(
            flops=8 * rows * rows * HD, bytes_accessed=12 * rows * HD, transcendentals=2 * rows * rows
        ),
    )(slopes, bases, queries, first, second)


def per_device(q_self, k_self, v_self, q_cross, k_cross, v_cross, scale_exps, cross_slopes, offsets):
    rows = q_self.shape[1]
    seat = lax.axis_index("seq")
    tower = lax.axis_index("tower")
    y, high, x = seat // (NH * NX), (seat // NX) % NH, seat % NX
    place = y * NX + x
    crossing = place >= HALF
    z = high * NZ + tower // 2
    towers = lax.axis_size("tower")
    partner = jnp.bitwise_xor(tower, towers // 2)

    def heads_of(matrix):
        return matrix[0].reshape(rows, HALF, PER, HD)

    bound = jnp.exp2(scale_exps[0].astype(jnp.float32)).astype(jnp.bfloat16) * jnp.bfloat16(TOP)
    bound = bound.reshape(2, 1, HALF, PER, 1)
    kc = jnp.clip(heads_of(k_cross), -bound[0], bound[0])
    vc = jnp.clip(heads_of(v_cross), -bound[1], bound[1])
    ks, vs, qs, qc = heads_of(k_self), heads_of(v_self), heads_of(q_self), heads_of(q_cross)

    def pair(keys, values, chunk):
        both = jnp.stack([keys[:, :, chunk], values[:, :, chunk]], axis=2)
        return both.transpose(1, 0, 2, 3).reshape(HALF, rows, 2 * HD)

    def remote(seat_place):
        return NH * NZ // 2 if seat_place < HALF else 2

    def near(seat_place):
        return 0 if seat_place < HALF else -2

    mine = [pair(ks, vs, c) for c in range(PER)]
    other = [pair(kc, vc, c) for c in range(PER)]
    zs = move(mine[0], lambda p: 4)
    zm = move(other[0], lambda p: 2)
    zp = move(other[0], lambda p: -2)
    first, second = [None] * PER, [None] * PER
    for c in range(1, PER):
        block = spread(jnp.concatenate([mine[c], other[c]], axis=0))
        first[c] = move(block, remote)
        second[c] = move(block, near)
    queries = spread(
        jnp.concatenate([m.transpose(1, 0, 2, 3).reshape(HALF, rows, PER * HD) for m in (qs, qc)], axis=0)
    ).reshape(SEATS * rows, PER * HD)
    first[0] = spread(jnp.concatenate([zs, zm], axis=0))
    second[0] = spread(jnp.concatenate([mine[0], zp], axis=0))

    modality = tower // (towers // 2)
    head = jnp.maximum(place - HALF, 0) * PER
    slopes = lax.dynamic_slice(cross_slopes, (modality, head), (1, PER))[0]
    slopes = jnp.where(crossing, slopes * (LOG2E / (SEATS * NH * rows)), 0.0)
    shift = offsets[tower] - offsets[partner]
    run = NX * rows
    bases = jnp.stack(
        [(high - ((z + step) % (NH * NZ)) // NZ) * run + shift for step in (-2, 2)]
    ).astype(jnp.int32)
    outs = []
    for c in range(PER):
        out = attend(
            slopes, bases, queries,
            first[c].reshape(SEATS * rows, 2 * HD), second[c].reshape(SEATS * rows, 2 * HD), c,
        )
        outs.append(spread(out.reshape(SEATS, rows, HD)))
    full = jnp.stack(outs, axis=1).reshape(2, HALF, PER, rows, HD)
    full = full.transpose(0, 3, 1, 2, 4).reshape(2, 1, rows, HEADS * HD)
    return full[0], full[1]


def solution(mesh):
    split = P("tower", "seq", None)
    return jax.shard_map(
        per_device,
        mesh=mesh,
        in_specs=(split,) * 6 + (P("tower", None, None), P(), P()),
        out_specs=(split, split),
        check_vma=False,
    )
```

```python
import functools

import jax
import jax.numpy as jnp
import numpy as np
from jax import lax
from jax.experimental import pallas as pl
from jax.experimental.pallas import tpu as pltpu
from jax.sharding import PartitionSpec as P

HEADS = 24
HD = 128
TOP = 448.0
LOG2E = 1.4426950408889634

NY, NH, NX, NZ = 4, 2, 4, 4
SEATS = NY * NX
HALF = SEATS // 2
PER = HEADS // HALF
BOTH = ("seq", "tower")
VMEM_LIMIT = 32 * 1024 * 1024
PACK_LIMIT = 60 * 1024 * 1024


def z_route(pick):
    pairs = []
    around = NH * NZ
    for y in range(NY):
        for x in range(NX):
            for z in range(around):
                for core in range(2):

                    def device(at):
                        return (y * NH * NX + (at // NZ) * NX + x) * (2 * NZ) + (at % NZ) * 2 + core

                    pairs.append((device(z), device((z + pick(y * NX + x)) % around)))
    return pairs


def move(block, pick):
    return lax.ppermute(block, BOTH, z_route(pick))


def spread(block):
    groups = [[y * NH * NX + h * NX + x for y in range(NY) for x in range(NX)] for h in range(NH)]
    return lax.all_to_all(block, "seq", 0, 0, axis_index_groups=groups, tiled=True)


def attend_body(slope_ref, base_ref, q_ref, first_ref, second_ref, out_ref, tile_ref, score_ref, *, chunk, run, runs):
    step = pl.program_id(0)
    slope = slope_ref[chunk]

    @pl.when(step == 0)
    def _():
        rows = lax.broadcasted_iota(jnp.int32, (run, run), 0)
        cols = lax.broadcasted_iota(jnp.int32, (run, run), 1)
        tile_ref[...] = (rows - cols).astype(jnp.float32) * slope

    queries = q_ref[...]
    scale = HD ** (-0.5) * LOG2E
    peak = None
    for half, ref in enumerate((first_ref, second_ref)):
        for j in range(runs):
            scores = lax.dot_general(
                queries, ref[j * run : (j + 1) * run, :HD], (((1,), (1,)), ((), ())),
                preferred_element_type=jnp.float32,
            )
            base = ((step - j) * (2 * run) + base_ref[half]).astype(jnp.float32) * slope
            scores = scores * scale - jnp.abs(tile_ref[...] + base)
            at = (half * runs + j) * run
            score_ref[:, at : at + run] = scores
            for lane in range(0, run, 128):
                part = scores[:, lane : lane + 128]
                peak = part if peak is None else jnp.maximum(peak, part)
    peak = jnp.max(peak, axis=1, keepdims=True)
    total = jnp.zeros((run, 128), jnp.float32)
    out = jnp.zeros((run, HD), jnp.float32)
    for half, ref in enumerate((first_ref, second_ref)):
        for j in range(runs):
            at = (half * runs + j) * run
            weights = jnp.exp2(score_ref[:, at : at + run] - peak)
            for lane in range(0, run, 128):
                total = total + weights[:, lane : lane + 128]
            out = out + jnp.dot(
                weights.astype(jnp.bfloat16), ref[j * run : (j + 1) * run, HD:],
                preferred_element_type=jnp.float32,
            )
    out_ref[...] = (out / jnp.sum(total, axis=1, keepdims=True)).astype(jnp.bfloat16)


def attend(slopes, bases, queries, first, second, chunk, cols=(0, 0)):
    rows = queries.shape[0]
    runs = NY
    run = rows // runs
    at = queries.shape[1] // HD - PER + chunk
    return pl.pallas_call(
        functools.partial(attend_body, chunk=chunk, run=run, runs=runs),
        grid=(runs,),
        in_specs=[
            pl.BlockSpec(memory_space=pltpu.SMEM),
            pl.BlockSpec(memory_space=pltpu.SMEM),
            pl.BlockSpec((run, HD), lambda i: (i, at)),
            pl.BlockSpec((rows, 2 * HD), lambda i: (0, cols[0])),
            pl.BlockSpec((rows, 2 * HD), lambda i: (0, cols[1])),
        ],
        out_specs=pl.BlockSpec((run, HD), lambda i: (i, 0)),
        out_shape=jax.ShapeDtypeStruct((rows, HD), jnp.bfloat16),
        scratch_shapes=[
            pltpu.VMEM((run, run), jnp.float32),
            pltpu.VMEM((run, 2 * rows), jnp.float32),
        ],
        compiler_params=pltpu.CompilerParams(vmem_limit_bytes=VMEM_LIMIT),
        cost_estimate=pl.CostEstimate(
            flops=8 * rows * rows * HD, bytes_accessed=12 * rows * HD, transcendentals=2 * rows * rows
        ),
    )(slopes, bases, queries, first, second)


def pack_body(bound_ref, *refs, chunk, count):
    out_refs = refs[4 * count :]
    mine = out_refs[0]
    other = out_refs[1] if len(out_refs) > 1 else out_refs[0].at[HALF:]
    for c in range(count):
        ks_ref, vs_ref, kc_ref, vc_ref = refs[4 * c : 4 * c + 4]
        for j in range(HALF):
            cols = slice(j * HD, (j + 1) * HD)
            for kind, ref in enumerate((ks_ref, vs_ref)):
                mine[j, :, (2 * c + kind) * HD : (2 * c + kind + 1) * HD] = ref[:, cols]
            for kind, ref in enumerate((kc_ref, vc_ref)):
                top = bound_ref[kind, (chunk + c) * HALF + j]
                block = jnp.clip(ref[:, cols].astype(jnp.float32), -top, top)
                other[j, :, (2 * c + kind) * HD : (2 * c + kind + 1) * HD] = block.astype(jnp.bfloat16)


def pack(bounds, arrays, chunk, count, apart):
    rows = arrays[0].shape[0]
    outputs, seats = (2, HALF) if apart else (1, SEATS)
    shape = (seats, rows, count * 2 * HD)

    def source(c):
        return pl.BlockSpec((rows, HALF * HD), lambda i: (0, c))

    return pl.pallas_call(
        functools.partial(pack_body, chunk=chunk, count=count),
        grid=(1,),
        in_specs=[pl.BlockSpec(memory_space=pltpu.SMEM)] + [source(chunk + c) for c in range(count) for _ in range(4)],
        out_specs=[pl.BlockSpec(shape, lambda i: (0, 0, 0))] * outputs,
        out_shape=[jax.ShapeDtypeStruct(shape, jnp.bfloat16)] * outputs,
        compiler_params=pltpu.CompilerParams(vmem_limit_bytes=PACK_LIMIT),
    )(bounds, *(arrays * count))


def join_body(zs_ref, zm_ref, mine_ref, zp_ref, qs_ref, qc_ref, out_ref):
    for j in range(HALF):
        out_ref[j, :, : 2 * HD] = zs_ref[j]
        out_ref[HALF + j, :, : 2 * HD] = zm_ref[j]
        out_ref[j, :, 2 * HD : 4 * HD] = mine_ref[j]
        out_ref[HALF + j, :, 2 * HD : 4 * HD] = zp_ref[j]
        for c in range(PER):
            cols = slice((c * HALF + j) * HD, (c * HALF + j + 1) * HD)
            out_ref[j, :, (4 + c) * HD : (5 + c) * HD] = qs_ref[:, cols]
            out_ref[HALF + j, :, (4 + c) * HD : (5 + c) * HD] = qc_ref[:, cols]


def join(*arrays):
    rows = arrays[0].shape[1]
    shape = (SEATS, rows, (4 + PER) * HD)

    def whole(array_shape):
        return pl.BlockSpec(array_shape, lambda i: (0,) * len(array_shape))

    return pl.pallas_call(
        join_body,
        grid=(1,),
        in_specs=[whole(a.shape) for a in arrays],
        out_specs=whole(shape),
        out_shape=jax.ShapeDtypeStruct(shape, jnp.bfloat16),
        compiler_params=pltpu.CompilerParams(vmem_limit_bytes=VMEM_LIMIT),
    )(*arrays)


def unpack_body(*refs):
    self_ref, cross_ref = refs[PER:]
    for chunk in range(PER):
        for j in range(HALF):
            head = chunk * HALF + j
            cols = slice(head * HD, (head + 1) * HD)
            self_ref[:, cols] = refs[chunk][j]
            cross_ref[:, cols] = refs[chunk][HALF + j]


def unpack(*chunks):
    rows = chunks[0].shape[1]
    vmem = pl.BlockSpec(memory_space=pltpu.VMEM)
    return pl.pallas_call(
        unpack_body,
        in_specs=[vmem] * PER,
        out_specs=[vmem] * 2,
        out_shape=[jax.ShapeDtypeStruct((rows, HEADS * HD), jnp.bfloat16)] * 2,
        compiler_params=pltpu.CompilerParams(vmem_limit_bytes=VMEM_LIMIT),
    )(*chunks)


def after(value, *others):
    return lax.optimization_barrier((value,) + others)[0]


def per_device(q_self, k_self, v_self, q_cross, k_cross, v_cross, scale_exps, cross_slopes, offsets):
    rows = q_self.shape[1]
    seat = lax.axis_index("seq")
    tower = lax.axis_index("tower")
    y, high, x = seat // (NH * NX), (seat // NX) % NH, seat % NX
    place = y * NX + x
    crossing = place >= HALF
    z = high * NZ + tower // 2
    towers = lax.axis_size("tower")
    partner = jnp.bitwise_xor(tower, towers // 2)

    modality = tower // (towers // 2)
    slopes = cross_slopes.reshape(2, PER, HALF)[modality, :, place % HALF]
    slopes = jnp.where(crossing, slopes * (LOG2E / (SEATS * NH * rows)), 0.0)
    shift = offsets[tower] - offsets[partner]
    run = NX * rows
    bases = jnp.stack(
        [(high - ((z + step) % (NH * NZ)) // NZ) * run + shift for step in (-2, 2)]
    ).astype(jnp.int32)

    bounds = jnp.exp2(scale_exps[0].astype(jnp.float32)).astype(jnp.bfloat16).astype(jnp.float32) * TOP

    def remote(seat_place):
        return NH * NZ // 2 if seat_place < HALF else 2

    def near(seat_place):
        return 0 if seat_place < HALF else -2

    arrays = (k_self[0], v_self[0], k_cross[0], v_cross[0])
    mine, other = pack(bounds, arrays, 0, 1, True)
    zs = move(mine, lambda p: NH * NZ // 2)
    zm = move(other, lambda p: 2)
    zp = move(other, lambda p: -2)
    block = spread(pack(bounds, arrays, 1, 2, False)[0])
    zs, zm, zp, block = lax.optimization_barrier((zs, zm, zp, block))
    blocks = [block[:, :, : 2 * HD], block[:, :, 2 * HD :]]
    first, second = [move(blocks[0], remote)], [move(blocks[0], near)]
    joined = spread(join(zs, zm, mine, zp, q_self[0], q_cross[0]))
    last = blocks[1]
    first, second = first + [move(last, remote)], second + [move(last, near)]
    joined = joined.reshape(SEATS * rows, (4 + PER) * HD)
    outs = []
    for c in range(PER):
        if c:
            halves, cols = (a[c - 1].reshape(SEATS * rows, 2 * HD) for a in (first, second)), (0, 0)
        else:
            halves, cols = (joined, joined), (0, 1)
        out = attend(slopes, bases, joined, *halves, c, cols)
        outs.append(spread(out.reshape(SEATS, rows, HD)))
    mine, other = unpack(*outs)
    return mine[None], other[None]


def solution(mesh):
    split = P("tower", "seq", None)
    return jax.shard_map(
        per_device,
        mesh=mesh,
        in_specs=(split,) * 6 + (P("tower", None, None), P(), P()),
        out_specs=(split, split),
        check_vma=False,
    )
```

```python
import functools

import jax
import jax.numpy as jnp
import numpy as np
from jax import lax
from jax.experimental import pallas as pl
from jax.experimental.pallas import tpu as pltpu
from jax.sharding import PartitionSpec as P

HEADS = 24
HD = 128
TOP = 448.0
LOG2E = 1.4426950408889634

NY, NH, NX, NZ = 4, 2, 4, 4
SEATS = NY * NX
HALF = SEATS // 2
PER = HEADS // HALF
BOTH = ("seq", "tower")
VMEM_LIMIT = 32 * 1024 * 1024
PACK_LIMIT = 60 * 1024 * 1024


def z_route(pick):
    pairs = []
    around = NH * NZ
    for y in range(NY):
        for x in range(NX):
            for z in range(around):
                for core in range(2):

                    def device(at):
                        return (y * NH * NX + (at // NZ) * NX + x) * (2 * NZ) + (at % NZ) * 2 + core

                    pairs.append((device(z), device((z + pick(y * NX + x)) % around)))
    return pairs


def move(block, pick):
    return lax.ppermute(block, BOTH, z_route(pick))


def spread(block):
    groups = [[y * NH * NX + h * NX + x for y in range(NY) for x in range(NX)] for h in range(NH)]
    return lax.all_to_all(block, "seq", 0, 0, axis_index_groups=groups, tiled=True)


def attend_body(slope_ref, base_ref, q_ref, *refs, chunk):
    key_refs, value_refs = refs[:2], refs[2:4]
    out_ref, tile_ref, score_ref = refs[-3:]
    if len(refs) > 7:
        out_ref[:, :HD] = refs[4][...]
    slope = slope_ref[chunk]
    rows = q_ref.shape[0]
    run = tile_ref.shape[0]
    runs = rows // run
    scale = HD ** (-0.5) * LOG2E
    tile_ref[...] = (
        lax.broadcasted_iota(jnp.int32, (run, run), 0) - lax.broadcasted_iota(jnp.int32, (run, run), 1)
    ).astype(jnp.float32) * (slope / scale)
    for i in range(runs):
        own = slice(i * run, (i + 1) * run)
        peak = None
        for half, ref in enumerate(key_refs):
            for j in range(runs):
                scores = lax.dot_general(
                    q_ref[own, :], ref[j * run : (j + 1) * run, :], (((1,), (1,)), ((), ())),
                    preferred_element_type=jnp.float32,
                )
                base = ((i - j) * (2 * run) + base_ref[half]).astype(jnp.float32) * (slope / scale)
                scores = scores - jnp.abs(tile_ref[...] + base)
                at = (half * runs + j) * run
                score_ref[i % 2, :, at : at + run] = scores
                for lane in range(0, run, 128):
                    part = scores[:, lane : lane + 128]
                    peak = part if peak is None else jnp.maximum(peak, part)
        peak = jnp.max(peak, axis=1, keepdims=True) * scale
        total = jnp.zeros((run, 128), jnp.float32)
        out = jnp.zeros((run, HD), jnp.float32)
        for half, ref in enumerate(value_refs):
            for j in range(runs):
                at = (half * runs + j) * run
                weights = jnp.exp2(score_ref[i % 2, :, at : at + run] * scale - peak)
                for lane in range(0, run, 128):
                    total = total + weights[:, lane : lane + 128]
                out = out + jnp.dot(
                    weights.astype(jnp.bfloat16), ref[j * run : (j + 1) * run, :],
                    preferred_element_type=jnp.float32,
                )
        out_ref[own, -HD:] = (out / jnp.sum(total, axis=1, keepdims=True)).astype(jnp.bfloat16)


def attend(slopes, bases, queries, keys, values, chunk, beside=()):
    rows = queries.shape[0]
    run = rows // NY
    wide = HD * (1 + len(beside))

    def column(at):
        return pl.BlockSpec((rows, HD), lambda i: (0, at))

    return pl.pallas_call(
        functools.partial(attend_body, chunk=chunk),
        grid=(1,),
        in_specs=[pl.BlockSpec(memory_space=pltpu.SMEM)] * 2
        + [column(queries.shape[1] // HD - PER + chunk)]
        + [column(at) for _, at in keys + values]
        + [column(0) for _ in beside],
        out_specs=pl.BlockSpec((rows, wide), lambda i: (0, 0)),
        out_shape=jax.ShapeDtypeStruct((rows, wide), jnp.bfloat16),
        scratch_shapes=[pltpu.VMEM((run, run), jnp.float32), pltpu.VMEM((2, run, 2 * rows), jnp.float32)],
        compiler_params=pltpu.CompilerParams(vmem_limit_bytes=VMEM_LIMIT),
        cost_estimate=pl.CostEstimate(flops=rows * HD, bytes_accessed=rows * HD, transcendentals=0),
    )(slopes, bases, queries, *(a.reshape(rows, -1) for a, _ in keys + values), *beside)


def pack_body(exps_ref, *refs, items, outputs):
    out_refs = refs[len(refs) - outputs :]
    mine = out_refs[0]
    other = out_refs[1] if outputs > 1 else out_refs[0].at[HALF:]
    for n, (kind, chunk) in enumerate(items):
        self_ref, cross_ref = refs[2 * n : 2 * n + 2]
        to = slice(n * HD, (n + 1) * HD)
        for j in range(HALF):
            cols = slice(j * HD, (j + 1) * HD)
            mine[j, :, to] = self_ref[:, cols]
            block = cross_ref[:, cols]
            if kind is not None:
                power = jnp.full((1, HD), exps_ref[kind, chunk * HALF + j], jnp.int32)
                top = jnp.exp2(power.astype(jnp.float32)).astype(jnp.bfloat16).astype(jnp.float32) * TOP
                block = jnp.clip(block.astype(jnp.float32), -top, top).astype(jnp.bfloat16)
            other[j, :, to] = block


def pack(exps, pairs, items, apart=False):
    rows = pairs[0][0].shape[0]
    outputs, seats = (2, HALF) if apart else (1, SEATS)
    shape = (seats, rows, len(items) * HD)

    def slab(chunk):
        return pl.BlockSpec((rows, HALF * HD), lambda i: (0, chunk))

    return pl.pallas_call(
        functools.partial(pack_body, items=items, outputs=outputs),
        grid=(1,),
        in_specs=[pl.BlockSpec(memory_space=pltpu.SMEM)] + [slab(chunk) for _, chunk in items for _ in range(2)],
        out_specs=[pl.BlockSpec(shape, lambda i: (0, 0, 0))] * outputs,
        out_shape=[jax.ShapeDtypeStruct(shape, jnp.bfloat16)] * outputs,
        compiler_params=pltpu.CompilerParams(vmem_limit_bytes=PACK_LIMIT if len(items) < 5 else VMEM_LIMIT),
    )(exps, *(a for kind, _ in items for a in pairs[kind]))


def join_body(zs_ref, zm_ref, mine_ref, zp_ref, out_ref):
    for j in range(HALF):
        out_ref[j, :, :HD] = zs_ref[j]
        out_ref[HALF + j, :, :HD] = zm_ref[j]
        out_ref[j, :, HD:] = mine_ref[j]
        out_ref[HALF + j, :, HD:] = zp_ref[j]


def join(*arrays):
    _, rows, _ = arrays[0].shape
    shape = (SEATS, rows, 2 * HD)
    return pl.pallas_call(
        join_body,
        grid=(1,),
        in_specs=[pl.BlockSpec((HALF, rows, HD), lambda i: (0, 0, 0))] * 4,
        out_specs=pl.BlockSpec(shape, lambda i: (0, 0, 0)),
        out_shape=jax.ShapeDtypeStruct(shape, jnp.bfloat16),
        compiler_params=pltpu.CompilerParams(vmem_limit_bytes=VMEM_LIMIT),
        cost_estimate=pl.CostEstimate(flops=rows * HD, bytes_accessed=rows * HD, transcendentals=0),
    )(*arrays)


def unpack_body(*refs):
    self_ref, cross_ref = refs[-2:]
    chunk = 0
    for ref in refs[:-2]:
        for col in range(0, ref.shape[2], HD):
            for j in range(HALF):
                head = chunk * HALF + j
                cols = slice(head * HD, (head + 1) * HD)
                self_ref[:, cols] = ref[j, :, col : col + HD]
                cross_ref[:, cols] = ref[HALF + j, :, col : col + HD]
            chunk += 1


def unpack(*chunks):
    rows = chunks[0].shape[1]
    vmem = pl.BlockSpec(memory_space=pltpu.VMEM)
    return pl.pallas_call(
        unpack_body,
        in_specs=[vmem] * len(chunks),
        out_specs=[vmem] * 2,
        out_shape=[jax.ShapeDtypeStruct((rows, HEADS * HD), jnp.bfloat16)] * 2,
        compiler_params=pltpu.CompilerParams(vmem_limit_bytes=VMEM_LIMIT),
    )(*chunks)


def after(value, *others):
    return lax.optimization_barrier((value,) + others)[0]


def per_device(q_self, k_self, v_self, q_cross, k_cross, v_cross, scale_exps, cross_slopes, offsets):
    rows = q_self.shape[1]
    seat = lax.axis_index("seq")
    tower = lax.axis_index("tower")
    y, high, x = seat // (NH * NX), (seat // NX) % NH, seat % NX
    place = y * NX + x
    crossing = place >= HALF
    z = high * NZ + tower // 2
    towers = lax.axis_size("tower")
    partner = jnp.bitwise_xor(tower, towers // 2)

    modality = tower // (towers // 2)
    slopes = cross_slopes.reshape(2, PER, HALF)[modality, :, place % HALF]
    slopes = jnp.where(crossing, slopes * (LOG2E / (SEATS * NH * rows)), 0.0)
    shift = offsets[tower] - offsets[partner]
    run = NX * rows
    bases = jnp.stack(
        [(high - ((z + step) % (NH * NZ)) // NZ) * run + shift for step in (-2, 2)]
    ).astype(jnp.int32)

    def remote(seat_place):
        return NH * NZ // 2 if seat_place < HALF else 2

    def near(seat_place):
        return 0 if seat_place < HALF else -2

    exps = scale_exps[0]
    pairs = {0: (k_self[0], k_cross[0]), 1: (v_self[0], v_cross[0]), None: (q_self[0], q_cross[0])}
    mine, other = pack(exps, pairs, ((0, 0),), apart=True)
    zs = move(mine, lambda p: NH * NZ // 2)
    zm = move(other, lambda p: 2)
    zp = move(other, lambda p: -2)
    near_part = spread(pack(after(exps, mine), pairs, ((1, 0), (0, 1), (1, 1)))[0])
    far_part = pack(exps, pairs, ((0, 2), (1, 2), (None, 0), (None, 1), (None, 2)))[0]
    far_part = spread(after(far_part, near_part, zs, zm, zp))
    early = move(near_part, remote), move(near_part, near)
    joined = spread(after(join(zs, zm, mine, zp), far_part))
    block = far_part[:, :, : 2 * HD]
    late = move(after(block, joined, early[0]), remote), move(after(block, joined, early[1]), near)
    queries = far_part.reshape(SEATS * rows, -1)

    def shape(out):
        return out.reshape(SEATS, rows, -1)

    def halves(pair, at):
        return [(array, at) for array in pair]

    head = attend(slopes, bases, queries, [(joined, 0), (joined, 1)], halves(early, 0), 0)
    both = attend(slopes, bases, queries, halves(early, 1), halves(early, 2), 1, (head,))
    both_back = spread(after(shape(both), joined))
    tail = attend(after(slopes, both), bases, queries, halves(late, 0), halves(late, 1), 2)
    tail_back = spread(after(shape(tail), both_back))
    mine, other = unpack(both_back, tail_back)
    return mine[None], other[None]


def solution(mesh):
    split = P("tower", "seq", None)
    return jax.shard_map(
        per_device,
        mesh=mesh,
        in_specs=(split,) * 6 + (P("tower", None, None), P(), P()),
        out_specs=(split, split),
        check_vma=False,
    )
```

```python
import functools

import jax
import jax.numpy as jnp
import numpy as np
from jax import lax
from jax.experimental import pallas as pl
from jax.experimental.pallas import tpu as pltpu
from jax.sharding import PartitionSpec as P

HEADS = 24
HD = 128
TOP = 448.0
LOG2E = 1.4426950408889634

NY, NH, NX, NZ = 4, 2, 4, 4
SEATS = NY * NX
HALF = SEATS // 2
PER = HEADS // HALF
BOTH = ("seq", "tower")
VMEM_LIMIT = 20 * 1024 * 1024
PACK_LIMIT = 60 * 1024 * 1024


def z_route(pick):
    pairs = []
    around = NH * NZ
    for y in range(NY):
        for x in range(NX):
            for z in range(around):
                for core in range(2):

                    def device(at):
                        return (y * NH * NX + (at // NZ) * NX + x) * (2 * NZ) + (at % NZ) * 2 + core

                    pairs.append((device(z), device((z + pick(y * NX + x)) % around)))
    return pairs


def move(block, pick):
    return lax.ppermute(block, BOTH, z_route(pick))


def spread(block):
    groups = [[y * NH * NX + h * NX + x for y in range(NY) for x in range(NX)] for h in range(NH)]
    return lax.all_to_all(block, "seq", 0, 0, axis_index_groups=groups, tiled=True)


def attend_body(slope_ref, base_ref, q_ref, *refs, chunk):
    key_refs, value_refs = refs[:2], refs[2:4]
    out_ref, tile_ref, score_ref = refs[-3:]
    if len(refs) > 7:
        out_ref[:, :HD] = refs[4][...]
    slope = slope_ref[chunk]
    rows = q_ref.shape[0]
    run = tile_ref.shape[0]
    runs = rows // run
    scale = HD ** (-0.5) * LOG2E
    tile_ref[...] = (
        lax.broadcasted_iota(jnp.int32, (run, run), 0) - lax.broadcasted_iota(jnp.int32, (run, run), 1)
    ).astype(jnp.float32) * (slope / scale)
    for i in range(runs):
        own = slice(i * run, (i + 1) * run)
        peak = None
        for half, ref in enumerate(key_refs):
            for j in range(runs):
                scores = lax.dot_general(
                    q_ref[own, :], ref[j * run : (j + 1) * run, :], (((1,), (1,)), ((), ())),
                    preferred_element_type=jnp.float32,
                )
                base = ((i - j) * (2 * run) + base_ref[half]).astype(jnp.float32) * (slope / scale)
                scores = scores - jnp.abs(tile_ref[...] + base)
                at = (half * runs + j) * run
                score_ref[i % 2, :, at : at + run] = scores
                for lane in range(0, run, 128):
                    part = scores[:, lane : lane + 128]
                    peak = part if peak is None else jnp.maximum(peak, part)
        peak = jnp.max(peak, axis=1, keepdims=True) * scale
        total = jnp.zeros((run, 128), jnp.float32)
        out = jnp.zeros((run, HD), jnp.float32)
        for half, ref in enumerate(value_refs):
            for j in range(runs):
                at = (half * runs + j) * run
                weights = jnp.exp2(score_ref[i % 2, :, at : at + run] * scale - peak)
                for lane in range(0, run, 128):
                    total = total + weights[:, lane : lane + 128]
                out = out + jnp.dot(
                    weights.astype(jnp.bfloat16), ref[j * run : (j + 1) * run, :],
                    preferred_element_type=jnp.float32,
                )
        out_ref[own, -HD:] = (out / jnp.sum(total, axis=1, keepdims=True)).astype(jnp.bfloat16)


def attend(slopes, bases, queries, keys, values, chunk, beside=()):
    rows = queries.shape[0]
    run = rows // NY
    wide = HD * (1 + len(beside))

    def column(at):
        return pl.BlockSpec((rows, HD), lambda i: (0, at))

    return pl.pallas_call(
        functools.partial(attend_body, chunk=chunk),
        grid=(1,),
        in_specs=[pl.BlockSpec(memory_space=pltpu.SMEM)] * 2
        + [column(queries.shape[1] // HD - PER + chunk)]
        + [column(at) for _, at in keys + values]
        + [column(0) for _ in beside],
        out_specs=pl.BlockSpec((rows, wide), lambda i: (0, 0)),
        out_shape=jax.ShapeDtypeStruct((rows, wide), jnp.bfloat16),
        scratch_shapes=[pltpu.VMEM((run, run), jnp.float32), pltpu.VMEM((2, run, 2 * rows), jnp.float32)],
        compiler_params=pltpu.CompilerParams(vmem_limit_bytes=VMEM_LIMIT),
        cost_estimate=pl.CostEstimate(flops=rows * HD, bytes_accessed=rows * HD, transcendentals=0),
    )(slopes, bases, queries, *(a.reshape(rows, -1) for a, _ in keys + values), *beside)


def pack_body(exps_ref, *refs, items, outputs):
    out_refs = refs[len(refs) - outputs :]
    mine = out_refs[0]
    other = out_refs[1] if outputs > 1 else out_refs[0].at[HALF:]
    for n, (kind, chunk) in enumerate(items):
        self_ref, cross_ref = refs[2 * n : 2 * n + 2]
        to = slice(n * HD, (n + 1) * HD)
        for j in range(HALF):
            cols = slice(j * HD, (j + 1) * HD)
            mine[j, :, to] = self_ref[:, cols]
            block = cross_ref[:, cols]
            if kind is not None:
                power = jnp.full((1, HD), exps_ref[kind, chunk * HALF + j], jnp.int32)
                top = jnp.exp2(power.astype(jnp.float32)).astype(jnp.bfloat16).astype(jnp.float32) * TOP
                block = jnp.clip(block.astype(jnp.float32), -top, top).astype(jnp.bfloat16)
            other[j, :, to] = block


def pack(exps, pairs, items, apart=False):
    rows = pairs[0][0].shape[0]
    outputs, seats = (2, HALF) if apart else (1, SEATS)
    shape = (seats, rows, len(items) * HD)

    def slab(chunk):
        return pl.BlockSpec((rows, HALF * HD), lambda i: (0, chunk))

    return pl.pallas_call(
        functools.partial(pack_body, items=items, outputs=outputs),
        grid=(1,),
        in_specs=[pl.BlockSpec(memory_space=pltpu.SMEM)] + [slab(chunk) for _, chunk in items for _ in range(2)],
        out_specs=[pl.BlockSpec(shape, lambda i: (0, 0, 0))] * outputs,
        out_shape=[jax.ShapeDtypeStruct(shape, jnp.bfloat16)] * outputs,
        compiler_params=pltpu.CompilerParams(vmem_limit_bytes=PACK_LIMIT if len(items) < 5 else VMEM_LIMIT),
    )(exps, *(a for kind, _ in items for a in pairs[kind]))


def join_body(zs_ref, zm_ref, mine_ref, zp_ref, out_ref):
    for j in range(HALF):
        out_ref[j, :, :HD] = zs_ref[j]
        out_ref[HALF + j, :, :HD] = zm_ref[j]
        out_ref[j, :, HD:] = mine_ref[j]
        out_ref[HALF + j, :, HD:] = zp_ref[j]


def join(*arrays):
    _, rows, _ = arrays[0].shape
    shape = (SEATS, rows, 2 * HD)
    return pl.pallas_call(
        join_body,
        grid=(1,),
        in_specs=[pl.BlockSpec((HALF, rows, HD), lambda i: (0, 0, 0))] * 4,
        out_specs=pl.BlockSpec(shape, lambda i: (0, 0, 0)),
        out_shape=jax.ShapeDtypeStruct(shape, jnp.bfloat16),
        compiler_params=pltpu.CompilerParams(vmem_limit_bytes=VMEM_LIMIT),
        cost_estimate=pl.CostEstimate(flops=rows * HD, bytes_accessed=rows * HD, transcendentals=0),
    )(*arrays)


def unpack_body(back_ref, *refs):
    self_ref, cross_ref = refs[-2:]
    for c in range(back_ref.shape[2] // HD):
        for j in range(HALF):
            cols = slice((c * HALF + j) * HD, (c * HALF + j + 1) * HD)
            self_ref[:, cols] = back_ref[j, :, c * HD : (c + 1) * HD]
            cross_ref[:, cols] = back_ref[HALF + j, :, c * HD : (c + 1) * HD]


def unpack(back, at, partial=()):
    _, rows, wide = back.shape
    return pl.pallas_call(
        unpack_body,
        grid=(1,),
        in_specs=[pl.BlockSpec(back.shape, lambda i: (0, 0, 0))] + [pl.BlockSpec(memory_space=pl.ANY)] * len(partial),
        out_specs=[pl.BlockSpec((rows, wide * HALF), lambda i: (0, at))] * 2,
        out_shape=[jax.ShapeDtypeStruct((rows, HEADS * HD), jnp.bfloat16)] * 2,
        input_output_aliases={1: 0, 2: 1} if partial else {},
        compiler_params=pltpu.CompilerParams(vmem_limit_bytes=VMEM_LIMIT),
        cost_estimate=pl.CostEstimate(flops=rows * HD, bytes_accessed=rows * HD, transcendentals=0),
    )(back, *partial)


def after(value, *others):
    return lax.optimization_barrier((value,) + others)[0]


def per_device(q_self, k_self, v_self, q_cross, k_cross, v_cross, scale_exps, cross_slopes, offsets):
    rows = q_self.shape[1]
    seat = lax.axis_index("seq")
    tower = lax.axis_index("tower")
    y, high, x = seat // (NH * NX), (seat // NX) % NH, seat % NX
    place = y * NX + x
    crossing = place >= HALF
    z = high * NZ + tower // 2
    towers = lax.axis_size("tower")
    partner = jnp.bitwise_xor(tower, towers // 2)

    modality = tower // (towers // 2)
    slopes = cross_slopes.reshape(2, PER, HALF)[modality, :, place % HALF]
    slopes = jnp.where(crossing, slopes * (LOG2E / (SEATS * NH * rows)), 0.0)
    shift = offsets[tower] - offsets[partner]
    run = NX * rows
    bases = jnp.stack(
        [(high - ((z + step) % (NH * NZ)) // NZ) * run + shift for step in (-2, 2)]
    ).astype(jnp.int32)

    def remote(seat_place):
        return NH * NZ // 2 if seat_place < HALF else 2

    def near(seat_place):
        return 0 if seat_place < HALF else -2

    exps = scale_exps[0]
    pairs = {0: (k_self[0], k_cross[0]), 1: (v_self[0], v_cross[0]), None: (q_self[0], q_cross[0])}
    mine, other = pack(exps, pairs, ((0, 0),), apart=True)
    zs = move(mine, lambda p: NH * NZ // 2)
    zm = move(other, lambda p: 2)
    zp = move(other, lambda p: -2)
    near_part = spread(pack(after(exps, mine), pairs, ((1, 0), (0, 1), (1, 1)))[0])
    far_part = pack(exps, pairs, ((0, 2), (1, 2), (None, 0), (None, 1), (None, 2)))[0]
    far_part = spread(after(far_part, near_part, zs, zm, zp))
    early = move(near_part, remote), move(near_part, near)
    joined = spread(after(join(zs, zm, mine, zp), far_part))
    block = far_part[:, :, : 2 * HD]
    late = move(after(block, joined, early[0]), remote), move(after(block, joined, early[1]), near)
    queries = far_part.reshape(SEATS * rows, -1)

    def shape(out):
        return out.reshape(SEATS, rows, -1)

    def halves(pair, at):
        return [(array, at) for array in pair]

    head = attend(slopes, bases, queries, [(joined, 0), (joined, 1)], halves(early, 0), 0)
    both = attend(slopes, bases, queries, halves(early, 1), halves(early, 2), 1, (head,))
    both_back = spread(after(shape(both), joined))
    tail = attend(after(slopes, both), bases, queries, halves(late, 0), halves(late, 1), 2)
    tail_back = spread(after(shape(tail), both_back))
    mine, other = unpack(tail_back, PER - 1, unpack(both_back, 0))
    return mine[None], other[None]


def solution(mesh):
    split = P("tower", "seq", None)
    return jax.shard_map(
        per_device,
        mesh=mesh,
        in_specs=(split,) * 6 + (P("tower", None, None), P(), P()),
        out_specs=(split, split),
        check_vma=False,
    )
```
